256 devices in a mesh: dp: 16 (over x, z_lo), mp: 16 (over z_hi, y, core).
Axes of the slice: x: 4, y: 4, z: 8 (z_hi: 2, z_lo: 4; z = z_hi * 4 + z_lo), core: 2. Of those that a mesh axis runs over, the one named last changes fastest.
Arguments:
- acts: bfloat16 [2, 16384, 8192], P(None, 'dp', 'mp'), may hold values from -6 to 6
- out_grads: bfloat16 [2, 16384, 28672], P(None, 'dp', 'mp'), may hold values from -6 to 6
- token_ids: int32 [64, 256], P('dp'), may hold values from 0 to 128255
- lengths: int32 [64], P('dp'), may hold values from 64 to 256, as said below
- token_weight: float32 [128256], replicated, may hold values from 0.25 to 4
- proj_in: bfloat16 [2, 8192, 64], P(None, 'mp'), may hold values from -0.0625 to 0.0625
- proj_out: bfloat16 [2, 28672, 64], P(None, 'mp'), may hold values from -0.03125 to 0.03125
- hess_inv: float32 [2, 4096, 4096], P(None, 'mp', 'dp'), as said below
- queries: bfloat16 [2, 4096, 4096], P(None, 'dp', 'mp'), may hold values from -0.0078125 to 0.0078125
Outputs:
- scores: float32 [64, 4096], P('dp', 'mp')
The draws below stay inside these ranges and needn't reach their ends.
Inputs may be any that keep to these rules, and one draw needn't show every extreme that they name: `lengths`: some example uses all 256 slots. `hess_inv`: each layer's matrix is symmetric.
All inputs are finite; a program needn't handle non-finite values.
Results may differ from the reference program's by a relative error of at most 0.0003.
Values may be sent and summed in bfloat16 or wider, within the bound.
No kernel may reach another device: no remote copies, remote signals or barrier semaphores. Data moves between devices by JAX's collectives and lax.ppermute only.
A program may use at most 128 MiB of HBM per device.

```python
import math
import jax
import jax.numpy as jnp
import numpy as np
from jax import lax

D = 8192
FF = 28672
VOCAB = 128256
K = 64
LAYERS = 2
S = 256
F = 4096
EXAMPLES = 64
QUERIES = 4096
TOKENS = 16384


def draw_lengths(key, part):
    key = jax.random.fold_in(key, 11)
    drawn = jax.random.randint(key, (EXAMPLES,), S // 4, S + 1)
    chosen = jax.random.randint(jax.random.fold_in(key, 2), (), 0, EXAMPLES)
    return jnp.where(jnp.arange(EXAMPLES) == chosen, S, drawn).astype(jnp.int32)


def draw_hess_inv(key, part):
    key = jax.random.fold_in(key, 23)
    first, second = jax.random.split(key)
    entries = jax.random.normal(first, (LAYERS, F, F), jnp.float32)
    diagonal = jnp.exp(jax.random.uniform(second, (LAYERS, F), jnp.float32, -0.6931472, 0.6931472))
    offdiag = (entries + jnp.swapaxes(entries, 1, 2)) * (0.3 / F ** 0.5)
    rows = jnp.arange(F)[:, None]
    columns = jnp.arange(F)[None, :]
    eye_mask = (rows == columns).astype(jnp.float32)
    return offdiag * (1.0 - eye_mask) + eye_mask * diagonal[:, :, None]


def place_ends(result, own_key, smallest, high):
    shape = result.shape
    spot = [jax.random.randint(jax.random.fold_in(own_key, axis), (), 0, shape[axis]) for axis in range(len(shape))]
    result = result.at[tuple(spot)].set(smallest)
    longest = shape.index(max(shape))
    spot[longest] = (spot[longest] + 1) % shape[longest]
    return result.at[tuple(spot)].set(high)


def block_scale(key, extent, cuts, low, high):
    def one(axis_at, parts):
        heights = jax.random.uniform(jax.random.fold_in(jax.random.fold_in(key, 6), axis_at), (parts,), jnp.float32, low / len(cuts), high / len(cuts))
        return jnp.repeat(jnp.exp(heights), extent[axis_at] // parts).reshape((-1,) + (1,) * (len(extent) - axis_at - 1))

    gain = one(*cuts[0])
    for cut in cuts[1:]:
        gain = gain * one(*cut)
    return gain


def ranked_wide(rng, shape, number_of, slope):
    weights = [min(1 << octave, number_of + 1 - (1 << octave)) * (1 << 20) // math.isqrt((1 << octave) ** slope) + 1 for octave in range((number_of + 1).bit_length()) if 1 << octave <= number_of]
    width = 1 + sum(weights) // (1 << 30)
    listing = np.cumsum(np.array([max(1, weight // width) for weight in weights]))
    pick = jax.random.randint(jax.random.fold_in(rng, 1), shape, 0, int(listing[len(weights) - 1]))
    start = jnp.left_shift(1, jnp.searchsorted(jnp.asarray(listing, jnp.int32), pick, side="right").astype(jnp.int32))
    grade = start - 1 + jax.random.randint(jax.random.fold_in(rng, 4), shape, 0, 1 << 30) % jnp.minimum(start, number_of + 1 - start)
    return jax.random.permutation(jax.random.fold_in(rng, 2), number_of)[grade].astype(jnp.int32)


def gaussian(rng, shape, deviation, most, cuts=(), kind=jnp.bfloat16):
    values = deviation * jax.random.normal(rng, shape, jnp.float32)
    if cuts:
        values = values * block_scale(rng, shape, cuts, -0.22, 0.18)
    return jnp.clip(values, -most, most).astype(kind)


def setup_inputs(seed: int = 0) -> dict:
    seeds = jax.random.split(jax.random.key(seed), 10)
    acts = gaussian(seeds[0], (LAYERS, TOKENS, D), 1.0, 6.0, ((1, 16), (2, 16)))
    out_grads = gaussian(seeds[1], (LAYERS, TOKENS, FF), 1.0, 6.0, ((1, 16), (2, 16)))
    token_ids = place_ends(ranked_wide(seeds[2], (EXAMPLES, S), VOCAB, 2), jax.random.fold_in(seeds[2], 3), 0, VOCAB - 1).astype(jnp.int32)
    lengths = draw_lengths(jax.random.fold_in(seeds[9], 71), 0)
    token_weight = jnp.clip(jnp.exp(jax.random.uniform(seeds[4], (VOCAB,), jnp.float32, math.log(0.25), math.log(4.0))), 0.25, 4.0)
    proj_in = gaussian(seeds[5], (LAYERS, D, K), D ** -0.5, 0.0625, ((1, 16),))
    proj_out = gaussian(seeds[6], (LAYERS, FF, K), FF ** -0.5, 0.03125, ((1, 16),))
    hess_inv = draw_hess_inv(jax.random.fold_in(seeds[9], 71), 0)
    queries = gaussian(seeds[8], (LAYERS, QUERIES, F), (0.5 / (K * S ** 0.5)), 0.0078125, ((1, 16), (2, 16)))
    return {"acts": acts, "out_grads": out_grads, "token_ids": token_ids, "lengths": lengths, "token_weight": token_weight, "proj_in": proj_in, "proj_out": proj_out, "hess_inv": hess_inv, "queries": queries}


def reference(acts, out_grads, token_ids, lengths, token_weight, proj_in, proj_out, hess_inv, queries):
    positions = lax.broadcasted_iota(jnp.int32, (EXAMPLES, S), 1)
    weights = token_weight[token_ids] * (positions < lengths[:, None]).astype(jnp.float32)
    scores = jnp.zeros((EXAMPLES, QUERIES), jnp.float32)
    for layer in range(LAYERS):
        x_proj = jnp.dot(acts[layer], proj_in[layer], preferred_element_type=jnp.float32).reshape(EXAMPLES, S, K)
        g_proj = jnp.dot(out_grads[layer], proj_out[layer], preferred_element_type=jnp.float32).reshape(EXAMPLES, S, K)
        grams = jnp.einsum("esk,esj->ekj", x_proj * weights[:, :, None], g_proj, precision=lax.Precision.HIGHEST).reshape(EXAMPLES, F)
        image = jnp.dot(grams, hess_inv[layer], precision=lax.Precision.HIGHEST)
        scores = scores + jnp.dot(image, queries[layer].astype(jnp.float32).T, precision=lax.Precision.HIGHEST)
    return scores
```

```python
import functools
import jax
import jax.numpy as jnp
from jax import lax
from jax.experimental import pallas as pl
from jax.experimental.pallas import tpu as pltpu
from jax.sharding import PartitionSpec as P

AXES = ("dp", "mp")
VMEM = pl.BlockSpec(memory_space=pltpu.VMEM)
SMEM = pl.BlockSpec(memory_space=pltpu.SMEM)


def send(value, target):
    pairs = []
    for d in range(16):
        for m in range(16):
            td, tm = target(d, m)
            pairs.append((d * 16 + m, td * 16 + tm))
    return lax.ppermute(value, AXES, pairs)


def to_core(value):
    return send(value, lambda d, m: (d, m ^ 1))


def to_y(value, k):
    return send(value, lambda d, m: (d, m ^ (2 * k)))


def to_z(value):
    return send(value, lambda d, m: (d, m ^ 8))


def to_zl(value, k):
    return send(value, lambda d, m: (d ^ k, m))


def to_x(value, k):
    return send(value, lambda d, m: (d ^ (4 * k), m))


def project_kernel(layer_ref, acts_ref, grads_ref, in_ref, out_ref, res_ref):
    x = jnp.dot(acts_ref[0], in_ref[0], preferred_element_type=jnp.float32)
    g = jnp.dot(grads_ref[0], out_ref[0], preferred_element_type=jnp.float32)
    res_ref[...] = jnp.concatenate([x, g], axis=1)


def project(layer, acts, out_grads, proj_in, proj_out):
    tokens, width = acts.shape[1:]
    hidden = out_grads.shape[2]
    rank = proj_in.shape[2]
    block = 256
    return pl.pallas_call(
        project_kernel,
        grid_spec=pltpu.PrefetchScalarGridSpec(
            num_scalar_prefetch=1,
            grid=(tokens // block,),
            in_specs=[
                pl.BlockSpec((1, block, width), lambda t, l: (l[0], t, 0)),
                pl.BlockSpec((1, block, hidden), lambda t, l: (l[0], t, 0)),
                pl.BlockSpec((1, width, rank), lambda t, l: (l[0], 0, 0)),
                pl.BlockSpec((1, hidden, rank), lambda t, l: (l[0], 0, 0)),
            ],
            out_specs=pl.BlockSpec((block, 2 * rank), lambda t, l: (t, 0)),
        ),
        out_shape=jax.ShapeDtypeStruct((tokens, 2 * rank), jnp.float32),
        compiler_params=pltpu.CompilerParams(vmem_limit_bytes=32 * 2**20),
        cost_estimate=pl.CostEstimate(
            flops=2 * tokens * (width + hidden) * 256,
            bytes_accessed=tokens * (width + hidden) * 2,
            transcendentals=0,
        ),
    )(layer, acts, out_grads, proj_in, proj_out)


def call(kernel, out, *args, smem=1):
    return pl.pallas_call(
        kernel,
        in_specs=[SMEM] * smem + [VMEM] * (len(args) - smem),
        out_specs=[VMEM] * len(out),
        out_shape=[jax.ShapeDtypeStruct(s, jnp.float32) for s in out],
        compiler_params=pltpu.CompilerParams(vmem_limit_bytes=32 * 2**20),
    )(*args)


def split_kernel(place_ref, a_ref, b_ref, *outs):
    y = place_ref[1]
    rows = outs[0].shape[0]
    for k, out in enumerate(outs):
        at = pl.ds(pl.multiple_of((y ^ k) * rows, rows), rows)
        out[...] = a_ref[at] + b_ref[at]


def sum_kernel(place_ref, *refs):
    *ins, out = refs
    total = ins[0][...]
    for ref in ins[1:]:
        total = total + ref[...]
    out[...] = total


def gram_kernel(place_ref, a_ref, b_ref, w_ref, *refs):
    *outs, held = refs
    z, y = place_ref[0], place_ref[1]
    total = a_ref[...] + b_ref[...]
    x = total[:, :64] * w_ref[...]
    held[...] = lax.dot_general(
        x,
        total[:, 64:],
        (((0,), (0,)), ((), ())),
        precision=lax.Precision.HIGHEST,
        preferred_element_type=jnp.float32,
    )
    for k, out in enumerate(outs):
        out[...] = held[pl.ds(pl.multiple_of(z * 32 + (y ^ k) * 8, 8), 8)]


def image_kernel(place_ref, *refs):
    grams, hess = refs[:4], refs[4:8]
    out, held = refs[8:]
    y, c = place_ref[1], place_ref[2]
    for kz in range(4):
        for ky in range(4):
            held[:, pl.ds(4 * kz + (y ^ ky), 1), :] = grams[kz][ky][:, None, :]
    for block in range(2):
        at = (c ^ block) * 4
        rows = jnp.concatenate([held[at + i] for i in range(4)], axis=1)
        for k in range(4):
            part = jnp.dot(
                rows,
                hess[k][block],
                precision=lax.Precision.HIGHEST,
                preferred_element_type=jnp.float32,
            )
            cols = pl.ds(256 * k, 256)
            if block:
                out[:, cols] += part
            else:
                out[:, cols] = part


def score_kernel(place_ref, a_ref, b_ref, *refs):
    queries, outs = refs[:4], refs[4:]
    image = a_ref[...] + b_ref[...]
    high = image.astype(jnp.bfloat16)
    rest = image - high.astype(jnp.float32)
    mid = rest.astype(jnp.bfloat16)
    low = (rest - mid.astype(jnp.float32)).astype(jnp.bfloat16)
    rows = jnp.concatenate([high, mid, low], axis=0)
    count = image.shape[0]
    for block, out in enumerate(outs):
        total = 0.0
        for k in range(4):
            part = lax.dot_general(
                rows[:, 256 * k : 256 * (k + 1)],
                queries[k][block],
                (((1,), (1,)), ((), ())),
                preferred_element_type=jnp.float32,
            )
            total = total + (part[:count] + part[count : 2 * count] + part[2 * count :])
        out[...] = total


def per_device(
    acts, out_grads, token_ids, lengths, token_weight, proj_in, proj_out, hess_inv, queries
):
    m = lax.axis_index("mp")
    z, y, c = m >> 3, (m >> 1) & 3, m & 1
    place = jnp.stack([z, y, c]).astype(jnp.int32)
    f32 = jnp.float32

    other = project((1 - c)[None], acts, out_grads, proj_in, proj_out)
    theirs = to_core(other)
    mine = project(c[None], acts, out_grads, proj_in, proj_out)

    blocks = call(split_kernel, [(256, 128)] * 4, place, mine, theirs)
    got = [to_y(blocks[k], k) for k in (1, 2, 3)]

    hess_mine = lax.dynamic_index_in_dim(hess_inv, c, 0, keepdims=False)
    hess_theirs = to_core(lax.dynamic_index_in_dim(hess_inv, 1 - c, 0, keepdims=False))
    hess = jnp.stack([hess_mine, hess_theirs])
    hess = [hess] + [to_x(hess, k) for k in (1, 2, 3)]

    turned = send(queries, lambda d, m: (m, d))
    query_mine = lax.dynamic_index_in_dim(turned, c, 0, keepdims=False)
    query_theirs = to_core(lax.dynamic_index_in_dim(turned, 1 - c, 0, keepdims=False))
    query = jnp.stack([query_mine, query_theirs])
    query = [query] + [to_x(query, k) for k in (1, 2, 3)]

    ids = lax.dynamic_index_in_dim(token_ids, y, 0, keepdims=False)
    length = lax.dynamic_index_in_dim(lengths, y, 0, keepdims=False)
    live = (lax.iota(jnp.int32, ids.shape[0]) < length).astype(f32)
    weights = (token_weight[ids] * live)[:, None]

    (half,) = call(sum_kernel, [(256, 128)], place, blocks[0], *got)
    half_theirs = to_z(half)
    grams = pl.pallas_call(
        gram_kernel,
        in_specs=[SMEM] + [VMEM] * 3,
        out_specs=[VMEM] * 4,
        out_shape=[jax.ShapeDtypeStruct((8, 64), f32)] * 4,
        scratch_shapes=[pltpu.VMEM((64, 64), f32)],
    )(place, half, half_theirs, weights)
    rows = jnp.stack([grams[0]] + [to_y(grams[k], k) for k in (1, 2, 3)])
    rows = [rows] + [to_zl(rows, k) for k in (1, 2, 3)]

    image = pl.pallas_call(
        image_kernel,
        in_specs=[SMEM] + [VMEM] * 8,
        out_specs=VMEM,
        out_shape=jax.ShapeDtypeStruct((16, 1024), f32),
        scratch_shapes=[pltpu.VMEM((8, 16, 64), f32)],
        compiler_params=pltpu.CompilerParams(vmem_limit_bytes=32 * 2**20),
    )(place, *rows, *hess)
    got = [to_y(image, k) for k in (1, 2, 3)]
    (image,) = call(sum_kernel, [(16, 1024)], place, image, *got)
    image_theirs = to_z(image)
    keep, give = call(
        score_kernel, [(16, 256)] * 2, place, image, image_theirs, *query
    )
    scores = keep + to_core(give)
    result = scores[:4]
    for k in (1, 2, 3):
        result = result + to_zl(scores[4 * k : 4 * k + 4], k)
    return result


def solution(mesh):
    in_specs = (
        P(None, "dp", "mp"),
        P(None, "dp", "mp"),
        P("dp", None),
        P("dp"),
        P(),
        P(None, "mp", None),
        P(None, "mp", None),
        P(None, "mp", "dp"),
        P(None, "dp", "mp"),
    )
    out_specs = P("dp", "mp")
    return jax.shard_map(
        per_device, mesh=mesh, in_specs=in_specs, out_specs=out_specs, check_vma=False
    )
```

```python
import functools
import jax
import jax.numpy as jnp
from jax import lax
from jax.experimental import pallas as pl
from jax.experimental.pallas import tpu as pltpu
from jax.sharding import PartitionSpec as P

AXES = ("x", "zl", "z", "y", "c")
DP = ("x", "zl")
MP = ("z", "y", "c")
VMEM = pl.BlockSpec(memory_space=pltpu.VMEM)
SMEM = pl.BlockSpec(memory_space=pltpu.SMEM)
ANY = pl.BlockSpec(memory_space=pl.ANY)


def send(value, target):
    pairs = []
    for d in range(16):
        for m in range(16):
            td, tm = target(d, m)
            pairs.append((d * 16 + m, td * 16 + tm))
    return lax.ppermute(value, AXES, pairs)


def to_core(value):
    return send(value, lambda d, m: (d, m ^ 1))


def to_z(value):
    return send(value, lambda d, m: (d, m ^ 8))


def to_zl(value, k):
    return send(value, lambda d, m: (d ^ k, m))


def to_x(value, k):
    return send(value, lambda d, m: (d ^ (4 * k), m))


def where():
    return lax.axis_index("z"), lax.axis_index("y"), lax.axis_index("c")


def project_kernel(layer_ref, acts_ref, grads_ref, in_ref, out_ref, res_ref):
    def times(rows, weights):
        return lax.dot_general(
            rows, weights, (((1,), (1,)), ((), ())), preferred_element_type=jnp.float32
        )

    x = times(acts_ref[0], in_ref[0])
    g = times(grads_ref[0], out_ref[0])
    res_ref[...] = jnp.concatenate([x, g], axis=1)


def project(layer, acts, out_grads, proj_in, proj_out):
    tokens, width = acts.shape[1:]
    hidden = out_grads.shape[2]
    rank = proj_in.shape[1]
    block = 512
    return pl.pallas_call(
        project_kernel,
        grid_spec=pltpu.PrefetchScalarGridSpec(
            num_scalar_prefetch=1,
            grid=(tokens // block,),
            in_specs=[
                pl.BlockSpec((1, block, width), lambda t, l: (l[0], t, 0)),
                pl.BlockSpec((1, block, hidden), lambda t, l: (l[0], t, 0)),
                pl.BlockSpec((1, rank, width), lambda t, l: (l[0], 0, 0)),
                pl.BlockSpec((1, rank, hidden), lambda t, l: (l[0], 0, 0)),
            ],
            out_specs=pl.BlockSpec((block, 2 * rank), lambda t, l: (t, 0)),
        ),
        out_shape=jax.ShapeDtypeStruct((tokens, 2 * rank), jnp.float32),
        compiler_params=pltpu.CompilerParams(vmem_limit_bytes=56 * 2**20),
        cost_estimate=pl.CostEstimate(
            flops=2 * tokens * (width + hidden) * 256,
            bytes_accessed=tokens * (width + hidden) * 2,
            transcendentals=0,
        ),
    )(layer, acts, out_grads, proj_in, proj_out)


def cost(us):
    return pl.CostEstimate(flops=0, bytes_accessed=int(us * 3.69e6), transcendentals=0)


def call(kernel, out, *args, scratch=(), specs=None, us=1.0):
    return pl.pallas_call(
        kernel,
        in_specs=specs or [VMEM] * len(args),
        out_specs=[VMEM] * len(out),
        out_shape=[jax.ShapeDtypeStruct(s, jnp.float32) for s in out],
        scratch_shapes=[pltpu.VMEM(s, jnp.float32) for s in scratch],
        cost_estimate=cost(us),
        compiler_params=pltpu.CompilerParams(vmem_limit_bytes=32 * 2**20),
    )(*args)


def split_kernel(a_ref, b_ref, out):
    rows = out.shape[1]
    for block in range(out.shape[0]):
        at = slice(rows * block, rows * (block + 1))
        out[block] = a_ref[at] + b_ref[at]


def total_kernel(parts_ref, out):
    out[...] = jnp.sum(parts_ref[...], axis=0)


def gram_kernel(length_ref, a_ref, b_ref, w_ref, out, held):
    x, y = lax.axis_index("x"), lax.axis_index("y")
    total = a_ref[...] + b_ref[...]
    slots = lax.broadcasted_iota(jnp.int32, w_ref.shape, 1)
    weights = jnp.where(slots < length_ref[y], w_ref[...], 0.0)
    held[...] = jnp.dot(
        total[:, :64].T * weights,
        total[:, 64:],
        precision=lax.Precision.HIGHEST,
        preferred_element_type=jnp.float32,
    )
    for zl in range(4):
        piece = []
        for k in range(4):
            at = (x ^ k) * 16 + zl * 4
            even = held[pl.ds(at, 2, stride=2)]
            odd = held[pl.ds(at + 1, 2, stride=2)]
            piece.append(jnp.concatenate([even, odd], axis=1))
        piece = jnp.concatenate(piece, axis=0)
        for core in range(2):
            for y in range(4):
                out[16 * core + 4 * zl + y] = piece


def image_kernel(rows_ref, *refs):
    hess, out = refs[:4], refs[4]
    for layer in range(2):
        at = slice(16 * layer, 16 * (layer + 1))
        total = 0.0
        for k in range(4):
            rows = [rows_ref[at, 2 * k + half, :] for half in range(2)]
            total = total + lax.dot_general(
                jnp.concatenate(rows, axis=1),
                hess[k][layer],
                (((1,), (1,)), ((), ())),
                precision=lax.Precision.HIGHEST,
                preferred_element_type=jnp.float32,
            )
        out[at] = total


def score_kernel(*refs):
    images, queries, out = refs[:4], refs[4:8], refs[8]
    x = lax.axis_index("x")
    image = images[0][...] + images[1][...] + images[2][...] + images[3][...]
    high = image.astype(jnp.bfloat16)
    rest = image - high.astype(jnp.float32)
    mid = rest.astype(jnp.bfloat16)
    low = (rest - mid.astype(jnp.float32)).astype(jnp.bfloat16)
    for k in range(4):
        part = 0.0
        for layer in range(2):
            at = slice(16 * layer, 16 * (layer + 1))
            part = part + lax.dot_general(
                jnp.concatenate([high[at], mid[at], low[at]], axis=0),
                queries[k][layer],
                (((1,), (1,)), ((), ())),
                preferred_element_type=jnp.float32,
            )
        part = part[:16] + part[16:32] + part[32:]
        for zl in range(4):
            out[4 * (x ^ k) + zl] = part[4 * zl : 4 * zl + 4]


def per_device(
    acts, out_grads, token_ids, lengths, token_weight, proj_in, proj_out, hess_inv, queries
):
    z, y, c = where()
    proj_in = jnp.swapaxes(proj_in, 1, 2)
    proj_out = jnp.swapaxes(proj_out, 1, 2)
    others = (1, 2, 3)

    other = project((1 - c)[None], acts, out_grads, proj_in, proj_out)
    theirs = to_core(other)
    hess = [hess_inv] + [to_x(hess_inv, k) for k in others]
    query = [queries] + [to_x(queries, k) for k in others]
    mine = project(c[None], acts, out_grads, proj_in, proj_out)

    (blocks,) = call(split_kernel, [(4, 256, 128)], mine, theirs)
    blocks = lax.all_to_all(blocks, "y", 0, 0, tiled=True)

    ids = lax.dynamic_index_in_dim(token_ids, y, 0, keepdims=False)
    weights = token_weight.at[ids].get(mode="promise_in_bounds")[None]

    (half,) = call(total_kernel, [(256, 128)], blocks)
    (grams,) = call(
        gram_kernel,
        [(32, 8, 128)],
        lengths,
        half,
        to_z(half),
        weights,
        scratch=[(64, 64)],
        specs=[SMEM] + [VMEM] * 3,
    )
    grams = lax.all_to_all(grams, ("c", "zl", "y"), 0, 0, tiled=True)
    (image,) = call(image_kernel, [(32, 256)], grams, *hess)
    images = [image] + [to_zl(image, k) for k in others]
    (parts,) = call(score_kernel, [(16, 4, 256)], *images, *query)
    parts = lax.all_to_all(parts, MP, 0, 0, tiled=True)
    (scores,) = call(total_kernel, [(4, 256)], parts)
    return send(scores, lambda d, m: (d // 4 * 4 + m % 4, m // 4 * 4 + d % 4))


def solution(mesh):
    mesh = jax.sharding.Mesh(mesh.devices.reshape(4, 4, 2, 4, 2), AXES)
    in_specs = (
        P(None, DP, MP),
        P(None, DP, MP),
        P(DP, None),
        P(DP),
        P(),
        P(None, MP, None),
        P(None, MP, None),
        P(None, MP, DP),
        P(None, DP, MP),
    )
    return jax.shard_map(
        per_device, mesh=mesh, in_specs=in_specs, out_specs=P(DP, MP), check_vma=False
    )
```

```python
import functools
import jax
import jax.numpy as jnp
from jax import lax
from jax.experimental import pallas as pl
from jax.experimental.pallas import tpu as pltpu
from jax.sharding import PartitionSpec as P

AXES = ("x", "zl", "z", "y", "c")
DP = ("x", "zl")
MP = ("z", "y", "c")
VMEM = pl.BlockSpec(memory_space=pltpu.VMEM)
SMEM = pl.BlockSpec(memory_space=pltpu.SMEM)
ANY = pl.BlockSpec(memory_space=pl.ANY)


def send(value, target):
    pairs = []
    for d in range(16):
        for m in range(16):
            td, tm = target(d, m)
            pairs.append((d * 16 + m, td * 16 + tm))
    return lax.ppermute(value, AXES, pairs)


def to_core(value):
    return send(value, lambda d, m: (d, m ^ 1))


def to_z(value):
    return send(value, lambda d, m: (d, m ^ 8))


def to_zl(value, k):
    return send(value, lambda d, m: (d ^ k, m))


def to_x(value, k):
    return send(value, lambda d, m: ((d + 4 * k) % 16, m))


def where():
    return lax.axis_index("z"), lax.axis_index("y"), lax.axis_index("c")


def project_kernel(layer_ref, acts_ref, grads_ref, in_ref, out_ref, res_ref):
    def times(rows, weights):
        return lax.dot_general(
            rows, weights, (((1,), (1,)), ((), ())), preferred_element_type=jnp.float32
        )

    x = times(acts_ref[0], in_ref[0])
    g = times(grads_ref[0], out_ref[0])
    res_ref[...] = jnp.concatenate([x, g], axis=1)


def project(layer, acts, out_grads, proj_in, proj_out):
    tokens, width = acts.shape[1:]
    hidden = out_grads.shape[2]
    rank = proj_in.shape[1]
    block = 512
    return pl.pallas_call(
        project_kernel,
        grid_spec=pltpu.PrefetchScalarGridSpec(
            num_scalar_prefetch=1,
            grid=(tokens // block,),
            in_specs=[
                pl.BlockSpec((1, block, width), lambda t, l: (l[0], t, 0)),
                pl.BlockSpec((1, block, hidden), lambda t, l: (l[0], t, 0)),
                pl.BlockSpec((1, rank, width), lambda t, l: (l[0], 0, 0)),
                pl.BlockSpec((1, rank, hidden), lambda t, l: (l[0], 0, 0)),
            ],
            out_specs=pl.BlockSpec((block, 2 * rank), lambda t, l: (t, 0)),
        ),
        out_shape=jax.ShapeDtypeStruct((tokens, 2 * rank), jnp.float32),
        compiler_params=pltpu.CompilerParams(vmem_limit_bytes=56 * 2**20),
        cost_estimate=pl.CostEstimate(
            flops=2 * tokens * (width + hidden) * 256,
            bytes_accessed=tokens * (width + hidden) * 2,
            transcendentals=0,
        ),
    )(layer, acts, out_grads, proj_in, proj_out)


def cost(us):
    return pl.CostEstimate(flops=0, bytes_accessed=int(us * 3.69e6), transcendentals=0)


def call(kernel, out, *args, scratch=(), specs=None, us=1.0):
    return pl.pallas_call(
        kernel,
        in_specs=specs or [VMEM] * len(args),
        out_specs=[VMEM] * len(out),
        out_shape=[jax.ShapeDtypeStruct(s, jnp.float32) for s in out],
        scratch_shapes=[
            pltpu.VMEM(s, jnp.float32) if isinstance(s, tuple) else s for s in scratch
        ],
        cost_estimate=cost(us),
        compiler_params=pltpu.CompilerParams(vmem_limit_bytes=12 * 2**20),
    )(*args)


def split_kernel(a_ref, b_ref, out):
    rows = out.shape[1]
    for block in range(out.shape[0]):
        at = slice(rows * block, rows * (block + 1))
        out[block] = a_ref[at] + b_ref[at]


def total_kernel(parts_ref, out):
    at = 16 * lax.rem(lax.axis_index("y"), 2) + 8 * lax.axis_index("c")
    out[...] = jnp.sum(parts_ref[pl.ds(at, 8)], axis=0)


def half_kernel(parts_ref, out):
    out[...] = jnp.sum(parts_ref[...], axis=0)


def gram_kernel(length_ref, a_ref, b_ref, w_ref, *refs):
    out, held = refs[-2:]
    x, y = lax.axis_index("x"), lax.axis_index("y")
    total = a_ref[...] + b_ref[...]
    slots = lax.broadcasted_iota(jnp.int32, w_ref.shape, 1)
    weights = jnp.where(slots < length_ref[y], w_ref[...], 0.0)
    inputs = (total[:, :64].T * weights).reshape(32, 2, -1)
    for odd in range(2):
        held[:, 64 * odd : 64 * (odd + 1)] = jnp.dot(
            inputs[:, odd],
            total[:, 64:],
            precision=lax.Precision.HIGHEST,
            preferred_element_type=jnp.float32,
        )
    for zl in range(4):
        piece = jnp.concatenate(
            [held[pl.ds(lax.rem(x + k, 4) * 8 + zl * 2, 2)] for k in (0, 3, 1, 2)], axis=0
        )
        for core in range(2):
            for y in range(4):
                out[16 * core + 4 * zl + y] = piece


def two_terms(value):
    high = value.astype(jnp.bfloat16)
    return high, (value - high.astype(jnp.float32)).astype(jnp.bfloat16)


def times(left, right):
    return lax.dot_general(
        left, right, (((1,), (1,)), ((), ())), preferred_element_type=jnp.float32
    )


def image_kernel(rows_ref, *refs):
    hess, out = refs[:4], refs[4]
    for layer in range(2):
        at = slice(16 * layer, 16 * (layer + 1))
        total = 0.0
        for k in range(4):
            rows = [rows_ref[at, 2 * k + half, :] for half in range(2)]
            high, low = two_terms(jnp.concatenate(rows, axis=1))
            right, rest = two_terms(hess[k][layer])
            both = times(jnp.concatenate([high, low], axis=0), right)
            total = total + (both[:16] + (both[16:] + times(high, rest)))
        out[at] = total


def score_kernel(*refs):
    images, queries = refs[:4], refs[4:8]
    keep, give, held = refs[8:]
    x, z = lax.axis_index("x"), lax.axis_index("z")
    image = images[0][...] + images[1][...] + images[2][...] + images[3][...]
    high, low = two_terms(image)
    for k, step in enumerate((0, 3, 1, 2)):
        part = 0.0
        for layer in range(2):
            at = slice(16 * layer, 16 * (layer + 1))
            part = part + times(
                jnp.concatenate([high[at], low[at]], axis=0), queries[k][layer]
            )
        part = part[:16] + part[16:]
        block = lax.rem(x + step, 4)
        for zl in range(4):
            held[(block >> 1) ^ z, 4 * (block & 1) + zl] = part[4 * zl : 4 * zl + 4]
    keep[...] = held[0]
    give[...] = held[1]


def place_kernel(a_ref, b_ref, out):
    here = lax.axis_index("zl")
    out[...] = jnp.zeros_like(out)
    for y in range(2):
        for zl in range(4):
            out[8 * zl + 4 * y + here] = a_ref[4 * y + zl] + b_ref[4 * y + zl]


def per_device(
    acts, out_grads, token_ids, lengths, token_weight, proj_in, proj_out, hess_inv, queries
):
    z, y, c = where()
    proj_in = jnp.swapaxes(proj_in, 1, 2)
    proj_out = jnp.swapaxes(proj_out, 1, 2)
    others = (1, 2, 3)

    other = project((1 - c)[None], acts, out_grads, proj_in, proj_out)
    theirs = to_core(other)
    hess = [hess_inv, to_x(hess_inv, 1), to_x(hess_inv, -1)]
    query = [queries, to_x(queries, 1), to_x(queries, -1)]
    hess.append(to_x(hess[1], 1))
    query.append(to_x(query[2], -1))
    mine = project(c[None], acts, out_grads, proj_in, proj_out)

    (blocks,) = call(split_kernel, [(4, 256, 128)], mine, theirs)
    blocks = lax.all_to_all(blocks, "y", 0, 0, tiled=True)

    ids = lax.dynamic_index_in_dim(token_ids, y, 0, keepdims=False)
    weights = token_weight.at[ids].get(mode="promise_in_bounds")[None]

    (half,) = call(half_kernel, [(256, 128)], blocks)
    (grams,) = call(
        gram_kernel,
        [(32, 8, 128)],
        lengths,
        half,
        to_z(half),
        weights,
        scratch=[(32, 128)],
        specs=[SMEM] + [VMEM] * 3,
    )
    grams = lax.all_to_all(grams, ("c", "zl", "y"), 0, 0, tiled=True)
    (image,) = call(image_kernel, [(32, 256)], grams, *hess)
    images = [image] + [to_zl(image, k) for k in others]
    keep, give = call(
        score_kernel, [(8, 4, 256)] * 2, *images, *query, scratch=[(2, 8, 4, 256)]
    )
    (parts,) = call(place_kernel, [(32, 4, 256)], keep, to_z(give))
    parts = lax.all_to_all(parts, ("zl", "y", "c"), 0, 0, tiled=True)
    (scores,) = call(total_kernel, [(4, 256)], parts)
    return scores


def solution(mesh):
    mesh = jax.sharding.Mesh(mesh.devices.reshape(4, 4, 2, 4, 2), AXES)
    in_specs = (
        P(None, DP, MP),
        P(None, DP, MP),
        P(DP, None),
        P(DP),
        P(),
        P(None, MP, None),
        P(None, MP, None),
        P(None, MP, DP),
        P(None, DP, MP),
    )
    return jax.shard_map(
        per_device, mesh=mesh, in_specs=in_specs, out_specs=P(DP, MP), check_vma=False
    )
```

```python
import functools
import jax
import jax.numpy as jnp
from jax import lax
from jax.experimental import pallas as pl
from jax.experimental.pallas import tpu as pltpu
from jax.sharding import PartitionSpec as P

AXES = ("x", "zl", "z", "y", "c")
DP = ("x", "zl")
MP = ("z", "y", "c")
VMEM = pl.BlockSpec(memory_space=pltpu.VMEM)
SMEM = pl.BlockSpec(memory_space=pltpu.SMEM)
ANY = pl.BlockSpec(memory_space=pl.ANY)


def send(value, target):
    pairs = []
    for d in range(16):
        for m in range(16):
            td, tm = target(d, m)
            pairs.append((d * 16 + m, td * 16 + tm))
    return lax.ppermute(value, AXES, pairs)


def to_core(value):
    return send(value, lambda d, m: (d, m ^ 1))


def to_z(value):
    return send(value, lambda d, m: (d, m ^ 8))


def to_zl(value, k):
    return send(value, lambda d, m: (d ^ k, m))


def to_x(value, k):
    return send(value, lambda d, m: ((d + 4 * k) % 16, m))


def where():
    return lax.axis_index("z"), lax.axis_index("y"), lax.axis_index("c")


def project_kernel(layer_ref, acts_ref, grads_ref, in_ref, out_ref, res_ref):
    def times(rows, weights):
        return lax.dot_general(
            rows, weights, (((1,), (1,)), ((), ())), preferred_element_type=jnp.float32
        )

    x = times(acts_ref[0], in_ref[0])
    g = times(grads_ref[0], out_ref[0])
    res_ref[...] = jnp.concatenate([x, g], axis=1)


def project(layer, acts, out_grads, proj_in, proj_out):
    tokens, width = acts.shape[1:]
    hidden = out_grads.shape[2]
    rank = proj_in.shape[1]
    block = 512
    return pl.pallas_call(
        project_kernel,
        grid_spec=pltpu.PrefetchScalarGridSpec(
            num_scalar_prefetch=1,
            grid=(tokens // block,),
            in_specs=[
                pl.BlockSpec((1, block, width), lambda t, l: (l[0], t, 0)),
                pl.BlockSpec((1, block, hidden), lambda t, l: (l[0], t, 0)),
                pl.BlockSpec((1, rank, width), lambda t, l: (l[0], 0, 0)),
                pl.BlockSpec((1, rank, hidden), lambda t, l: (l[0], 0, 0)),
            ],
            out_specs=pl.BlockSpec((block, 2 * rank), lambda t, l: (t, 0)),
        ),
        out_shape=jax.ShapeDtypeStruct((tokens, 2 * rank), jnp.float32),
        compiler_params=pltpu.CompilerParams(vmem_limit_bytes=56 * 2**20),
        cost_estimate=pl.CostEstimate(
            flops=2 * tokens * (width + hidden) * 256,
            bytes_accessed=tokens * (width + hidden) * 2,
            transcendentals=0,
        ),
    )(layer, acts, out_grads, proj_in, proj_out)


def cost(us):
    return pl.CostEstimate(flops=0, bytes_accessed=int(us * 3.69e6), transcendentals=0)


def call(kernel, out, *args, scratch=(), specs=None, us=1.0):
    return pl.pallas_call(
        kernel,
        in_specs=specs or [VMEM] * len(args),
        out_specs=[VMEM] * len(out),
        out_shape=[jax.ShapeDtypeStruct(s, jnp.float32) for s in out],
        scratch_shapes=[
            pltpu.VMEM(s, jnp.float32) if isinstance(s, tuple) else s for s in scratch
        ],
        cost_estimate=cost(us),
        compiler_params=pltpu.CompilerParams(vmem_limit_bytes=12 * 2**20),
    )(*args)


def split_kernel(a_ref, b_ref, out):
    rows = out.shape[1]
    for block in range(out.shape[0]):
        at = slice(rows * block, rows * (block + 1))
        out[block] = a_ref[at] + b_ref[at]


def total_kernel(parts_ref, out):
    at = 16 * lax.rem(lax.axis_index("y"), 2) + 8 * lax.axis_index("c")
    out[...] = jnp.sum(parts_ref[pl.ds(at, 8)], axis=0)


def half_kernel(parts_ref, out):
    out[...] = jnp.sum(parts_ref[...], axis=0)


def gram_kernel(length_ref, a_ref, b_ref, w_ref, *refs):
    out, held = refs[-2:]
    x, y = lax.axis_index("x"), lax.axis_index("y")
    total = a_ref[...] + b_ref[...]
    slots = lax.broadcasted_iota(jnp.int32, w_ref.shape, 1)
    weights = jnp.where(slots < length_ref[y], w_ref[...], 0.0)
    inputs = (total[:, :64].T * weights).reshape(32, 2, -1)
    for odd in range(2):
        held[:, 64 * odd : 64 * (odd + 1)] = jnp.dot(
            inputs[:, odd],
            total[:, 64:],
            precision=lax.Precision.HIGHEST,
            preferred_element_type=jnp.float32,
        )
    for zl in range(4):
        piece = jnp.concatenate(
            [held[pl.ds(lax.rem(x + k, 4) * 8 + zl * 2, 2)] for k in (0, 3, 1, 2)], axis=0
        )
        for core in range(2):
            for y in range(4):
                out[16 * core + 4 * zl + y] = piece


def two_terms(value):
    high = value.astype(jnp.bfloat16)
    return high, (value - high.astype(jnp.float32)).astype(jnp.bfloat16)


def times(left, right):
    return lax.dot_general(
        left, right, (((1,), (1,)), ((), ())), preferred_element_type=jnp.float32
    )


def image_kernel(rows_ref, *refs):
    hess, out = refs[:4], refs[4]
    for layer in range(2):
        at = slice(16 * layer, 16 * (layer + 1))
        total = 0.0
        for k in range(4):
            rows = [rows_ref[at, 2 * k + half, :] for half in range(2)]
            high, low = two_terms(jnp.concatenate(rows, axis=1))
            right, rest = two_terms(hess[k][layer])
            both = times(jnp.concatenate([high, low], axis=0), right)
            total = total + (both[:16] + (both[16:] + times(high, rest)))
        out[at] = total


def score_kernel(*refs):
    images, queries, out = refs[:4], refs[4:8], refs[8]
    x = lax.axis_index("x")
    image = images[0][...] + images[1][...] + images[2][...] + images[3][...]
    high, low = two_terms(image)
    for k, step in enumerate((0, 3, 1, 2)):
        part = 0.0
        for layer in range(2):
            at = slice(16 * layer, 16 * (layer + 1))
            part = part + times(
                jnp.concatenate([high[at], low[at]], axis=0), queries[k][layer]
            )
        part = part[:16] + part[16:]
        for zl in range(4):
            out[4 * lax.rem(x + step, 4) + zl] = part[4 * zl : 4 * zl + 4]


def place_kernel(a_ref, b_ref, out):
    here = lax.axis_index("zl") >> 1
    out[...] = jnp.zeros_like(out)
    for block in range(4):
        for zl in range(4):
            out[8 * zl + 2 * block + here] = a_ref[4 * block + zl] + b_ref[4 * block + zl]


def per_device(
    acts, out_grads, token_ids, lengths, token_weight, proj_in, proj_out, hess_inv, queries
):
    z, y, c = where()
    proj_in = jnp.swapaxes(proj_in, 1, 2)
    proj_out = jnp.swapaxes(proj_out, 1, 2)
    others = (1, 2, 3)

    other = project((1 - c)[None], acts, out_grads, proj_in, proj_out)
    theirs = to_core(other)
    hess = [hess_inv, to_x(hess_inv, 1), to_x(hess_inv, -1)]
    query = [queries, to_x(queries, 1), to_x(queries, -1)]
    hess.append(to_x(hess[1], 1))
    query.append(to_x(query[2], -1))
    mine = project(c[None], acts, out_grads, proj_in, proj_out)

    (blocks,) = call(split_kernel, [(4, 256, 128)], mine, theirs)
    blocks = lax.all_to_all(blocks, "y", 0, 0, tiled=True)

    ids = lax.dynamic_index_in_dim(token_ids, y, 0, keepdims=False)
    weights = token_weight.at[ids].get(mode="promise_in_bounds")[None]

    (half,) = call(half_kernel, [(256, 128)], blocks)
    (grams,) = call(
        gram_kernel,
        [(32, 8, 128)],
        lengths,
        half,
        to_z(half),
        weights,
        scratch=[(32, 128)],
        specs=[SMEM] + [VMEM] * 3,
    )
    grams = lax.all_to_all(grams, ("c", "zl", "y"), 0, 0, tiled=True)
    (image,) = call(image_kernel, [(32, 256)], grams, *hess)
    images = [image] + [to_zl(image, k) for k in others]
    (parts,) = call(score_kernel, [(16, 4, 256)], *images, *query)
    (parts,) = call(place_kernel, [(32, 4, 256)], parts, to_core(parts))
    parts = lax.all_to_all(parts, ("zl", "z", "y"), 0, 0, tiled=True)
    (scores,) = call(total_kernel, [(4, 256)], parts)
    return scores


def solution(mesh):
    mesh = jax.sharding.Mesh(mesh.devices.reshape(4, 4, 2, 4, 2), AXES)
    in_specs = (
        P(None, DP, MP),
        P(None, DP, MP),
        P(DP, None),
        P(DP),
        P(),
        P(None, MP, None),
        P(None, MP, None),
        P(None, MP, DP),
        P(None, DP, MP),
    )
    return jax.shard_map(
        per_device, mesh=mesh, in_specs=in_specs, out_specs=P(DP, MP), check_vma=False
    )
```

```python
import functools
import jax
import jax.numpy as jnp
from jax import lax
from jax.experimental import pallas as pl
from jax.experimental.pallas import tpu as pltpu
from jax.sharding import PartitionSpec as P

AXES = ("x", "zl", "z", "y", "c")
DP = ("x", "zl")
MP = ("z", "y", "c")
VMEM = pl.BlockSpec(memory_space=pltpu.VMEM)
SMEM = pl.BlockSpec(memory_space=pltpu.SMEM)
ANY = pl.BlockSpec(memory_space=pl.ANY)


def send(value, target):
    pairs = []
    for d in range(16):
        for m in range(16):
            td, tm = target(d, m)
            pairs.append((d * 16 + m, td * 16 + tm))
    return lax.ppermute(value, AXES, pairs)


def to_core(value):
    return send(value, lambda d, m: (d, m ^ 1))


def to_z(value):
    return send(value, lambda d, m: (d, m ^ 8))


def to_zl(value, k):
    return send(value, lambda d, m: (d ^ k, m))


def to_x(value, k):
    return send(value, lambda d, m: ((d + 4 * k) % 16, m))


def where():
    return lax.axis_index("z"), lax.axis_index("y"), lax.axis_index("c")


def project_kernel(layer_ref, acts_ref, grads_ref, in_ref, out_ref, res_ref):
    def times(rows, weights):
        return lax.dot_general(
            rows, weights, (((1,), (1,)), ((), ())), preferred_element_type=jnp.float32
        )

    x = times(acts_ref[0], in_ref[0])
    g = times(grads_ref[0], out_ref[0])
    res_ref[...] = jnp.concatenate([x, g], axis=1)


def project(layer, acts, out_grads, proj_in, proj_out, limit):
    tokens, width = acts.shape[1:]
    hidden = out_grads.shape[2]
    rank = proj_in.shape[1]
    block = 512
    return pl.pallas_call(
        project_kernel,
        grid_spec=pltpu.PrefetchScalarGridSpec(
            num_scalar_prefetch=1,
            grid=(tokens // block,),
            in_specs=[
                pl.BlockSpec((1, block, width), lambda t, l: (l[0], t, 0)),
                pl.BlockSpec((1, block, hidden), lambda t, l: (l[0], t, 0)),
                pl.BlockSpec((1, rank, width), lambda t, l: (l[0], 0, 0)),
                pl.BlockSpec((1, rank, hidden), lambda t, l: (l[0], 0, 0)),
            ],
            out_specs=pl.BlockSpec((block, 2 * rank), lambda t, l: (t, 0)),
        ),
        out_shape=jax.ShapeDtypeStruct((tokens, 2 * rank), jnp.float32),
        compiler_params=pltpu.CompilerParams(vmem_limit_bytes=limit * 2**20),
        cost_estimate=pl.CostEstimate(
            flops=2 * tokens * (width + hidden) * 256,
            bytes_accessed=tokens * (width + hidden) * 2,
            transcendentals=0,
        ),
    )(layer, acts, out_grads, proj_in, proj_out)


def cost(us):
    return pl.CostEstimate(flops=0, bytes_accessed=int(us * 3.69e6), transcendentals=0)


def call(kernel, out, *args, scratch=(), specs=None, us=1.0):
    return pl.pallas_call(
        kernel,
        in_specs=specs or [VMEM] * len(args),
        out_specs=[VMEM] * len(out),
        out_shape=[jax.ShapeDtypeStruct(s, jnp.float32) for s in out],
        scratch_shapes=[
            pltpu.VMEM(s, jnp.float32) if isinstance(s, tuple) else s for s in scratch
        ],
        cost_estimate=cost(us),
        compiler_params=pltpu.CompilerParams(vmem_limit_bytes=12 * 2**20),
    )(*args)


def split_kernel(a_ref, b_ref, out):
    rows = out.shape[1]
    for block in range(out.shape[0]):
        at = slice(rows * block, rows * (block + 1))
        out[block] = a_ref[at] + b_ref[at]


def total_kernel(parts_ref, out):
    at = 2 * lax.rem(lax.axis_index("y"), 2) + lax.axis_index("c")
    total = parts_ref[at]
    for k in range(1, 8):
        total = total + parts_ref[at + 4 * k]
    out[...] = total


def half_kernel(parts_ref, out):
    out[...] = jnp.sum(parts_ref[...], axis=0)


def gram_kernel(length_ref, a_ref, b_ref, w_ref, *refs):
    out, held = refs[-2:]
    x, y = lax.axis_index("x"), lax.axis_index("y")
    total = a_ref[...] + b_ref[...]
    slots = lax.broadcasted_iota(jnp.int32, w_ref.shape, 1)
    weights = jnp.where(slots < length_ref[y], w_ref[...], 0.0)
    inputs = (total[:, :64].T * weights).reshape(32, 2, -1)
    right, rest = two_terms(total[:, 64:])
    for odd in range(2):
        high, low = two_terms(inputs[:, odd])

        def dot(left, other):
            return jnp.dot(left, other, preferred_element_type=jnp.float32)

        held[:, 64 * odd : 64 * (odd + 1)] = dot(high, right) + (
            dot(low, right) + dot(high, rest)
        )
    for zl in range(4):
        piece = jnp.concatenate(
            [held[pl.ds(lax.rem(x + k, 4) * 8 + zl * 2, 2)] for k in (0, 3, 1, 2)], axis=0
        )
        for core in range(2):
            for y in range(4):
                out[16 * core + 4 * zl + y] = piece


def two_terms(value):
    high = value.astype(jnp.bfloat16)
    return high, (value - high.astype(jnp.float32)).astype(jnp.bfloat16)


def times(left, right):
    return lax.dot_general(
        left, right, (((1,), (1,)), ((), ())), preferred_element_type=jnp.float32
    )


def image_kernel(rows_ref, *refs):
    hess, out = refs[:4], refs[4]
    for layer in range(2):
        at = slice(16 * layer, 16 * (layer + 1))
        total = 0.0
        for k in range(4):
            rows = [rows_ref[at, 2 * k + half, :] for half in range(2)]
            high, low = two_terms(jnp.concatenate(rows, axis=1))
            right, rest = two_terms(hess[k][layer])
            both = times(jnp.concatenate([high, low], axis=0), right)
            total = total + (both[:16] + (both[16:] + times(high, rest)))
        out[at] = total


def score_kernel(*refs):
    images, queries, out = refs[:4], refs[4:8], refs[8]
    x = lax.axis_index("x")
    image = images[0][...] + images[1][...] + images[2][...] + images[3][...]
    high, low = two_terms(image)
    for k, step in enumerate((0, 3, 1, 2)):
        part = 0.0
        for layer in range(2):
            at = slice(16 * layer, 16 * (layer + 1))
            part = part + times(
                jnp.concatenate([high[at], low[at]], axis=0), queries[k][layer]
            )
        part = part[:16] + part[16:]
        for zl in range(4):
            out[4 * lax.rem(x + step, 4) + zl] = part[4 * zl : 4 * zl + 4]


def place_kernel(a_ref, b_ref, out):
    here = lax.axis_index("zl") >> 1
    out[...] = jnp.zeros_like(out)
    for block in range(4):
        for zl in range(4):
            out[16 * (block & 1) + 8 * here + 4 * (block >> 1) + zl] = a_ref[4 * block + zl] + b_ref[4 * block + zl]


def per_device(
    acts, out_grads, token_ids, lengths, token_weight, proj_in, proj_out, hess_inv, queries
):
    z, y, c = where()
    proj_in = jnp.swapaxes(proj_in, 1, 2)
    proj_out = jnp.swapaxes(proj_out, 1, 2)
    others = (1, 2, 3)

    other = project((1 - c)[None], acts, out_grads, proj_in, proj_out, 57)
    theirs = to_core(other)
    hess = [hess_inv, to_x(hess_inv, 1), to_x(hess_inv, -1)]
    query = [queries, to_x(queries, 1), to_x(queries, -1)]
    hess.append(to_x(hess[1], 1))
    query.append(to_x(query[2], -1))
    mine = project(c[None], acts, out_grads, proj_in, proj_out, 51)

    (blocks,) = call(split_kernel, [(4, 256, 128)], mine, theirs)
    blocks = lax.all_to_all(blocks, "y", 0, 0, tiled=True)

    ids = lax.dynamic_index_in_dim(token_ids, y, 0, keepdims=False)
    weights = token_weight.at[ids].get(mode="promise_in_bounds")[None]

    (half,) = call(half_kernel, [(256, 128)], blocks)
    (grams,) = call(
        gram_kernel,
        [(32, 8, 128)],
        lengths,
        half,
        to_z(half),
        weights,
        scratch=[(32, 128)],
        specs=[SMEM] + [VMEM] * 3,
    )
    grams = lax.all_to_all(grams, ("c", "zl", "y"), 0, 0, tiled=True)
    (image,) = call(image_kernel, [(32, 256)], grams, *hess)
    images = [image] + [to_zl(image, k) for k in others]
    (parts,) = call(score_kernel, [(16, 4, 256)], *images, *query)
    (parts,) = call(place_kernel, [(32, 4, 256)], parts, to_core(parts))
    parts = lax.all_to_all(parts, ("y", "z", "zl"), 0, 0, tiled=True)
    (scores,) = call(total_kernel, [(4, 256)], parts)
    return scores


def solution(mesh):
    mesh = jax.sharding.Mesh(mesh.devices.reshape(4, 4, 2, 4, 2), AXES)
    in_specs = (
        P(None, DP, MP),
        P(None, DP, MP),
        P(DP, None),
        P(DP),
        P(),
        P(None, MP, None),
        P(None, MP, None),
        P(None, MP, DP),
        P(None, DP, MP),
    )
    return jax.shard_map(
        per_device, mesh=mesh, in_specs=in_specs, out_specs=P(DP, MP), check_vma=False
    )
```

```python
import functools
import jax
import jax.numpy as jnp
from jax import lax
from jax.experimental import pallas as pl
from jax.experimental.pallas import tpu as pltpu
from jax.sharding import PartitionSpec as P

AXES = ("x", "zl", "z", "y", "c")
DP = ("x", "zl")
MP = ("z", "y", "c")
VMEM = pl.BlockSpec(memory_space=pltpu.VMEM)
SMEM = pl.BlockSpec(memory_space=pltpu.SMEM)
ANY = pl.BlockSpec(memory_space=pl.ANY)


def send(value, target):
    pairs = []
    for d in range(16):
        for m in range(16):
            td, tm = target(d, m)
            pairs.append((d * 16 + m, td * 16 + tm))
    return lax.ppermute(value, AXES, pairs)


def to_core(value):
    return send(value, lambda d, m: (d, m ^ 1))


def to_z(value):
    return send(value, lambda d, m: (d, m ^ 8))


def to_zl(value, k):
    return send(value, lambda d, m: (d ^ k, m))


def to_x(value, k):
    return send(value, lambda d, m: ((d + 4 * k) % 16, m))


def where():
    return lax.axis_index("z"), lax.axis_index("y"), lax.axis_index("c")


def project_kernel(layer_ref, acts_ref, grads_ref, in_ref, out_ref, res_ref):
    def times(rows, weights):
        return lax.dot_general(
            rows, weights, (((1,), (1,)), ((), ())), preferred_element_type=jnp.float32
        )

    x = times(acts_ref[0], in_ref[0])
    g = times(grads_ref[0], out_ref[0])
    res_ref[...] = jnp.concatenate([x, g], axis=1)


def project(layer, acts, out_grads, proj_in, proj_out, limit):
    tokens, width = acts.shape[1:]
    hidden = out_grads.shape[2]
    rank = proj_in.shape[1]
    block = 512
    return pl.pallas_call(
        project_kernel,
        grid_spec=pltpu.PrefetchScalarGridSpec(
            num_scalar_prefetch=1,
            grid=(tokens // block,),
            in_specs=[
                pl.BlockSpec((1, block, width), lambda t, l: (l[0], t, 0)),
                pl.BlockSpec((1, block, hidden), lambda t, l: (l[0], t, 0)),
                pl.BlockSpec((1, rank, width), lambda t, l: (l[0], 0, 0)),
                pl.BlockSpec((1, rank, hidden), lambda t, l: (l[0], 0, 0)),
            ],
            out_specs=pl.BlockSpec((block, 2 * rank), lambda t, l: (t, 0)),
        ),
        out_shape=jax.ShapeDtypeStruct((tokens, 2 * rank), jnp.float32),
        compiler_params=pltpu.CompilerParams(vmem_limit_bytes=limit * 2**20),
        cost_estimate=pl.CostEstimate(
            flops=2 * tokens * (width + hidden) * 256,
            bytes_accessed=tokens * (width + hidden) * 2,
            transcendentals=0,
        ),
    )(layer, acts, out_grads, proj_in, proj_out)


def cost(us):
    return pl.CostEstimate(flops=0, bytes_accessed=int(us * 3.69e6), transcendentals=0)


def call(kernel, out, *args, scratch=(), specs=None, us=1.0):
    return pl.pallas_call(
        kernel,
        in_specs=specs or [VMEM] * len(args),
        out_specs=[VMEM] * len(out),
        out_shape=[jax.ShapeDtypeStruct(s, jnp.float32) for s in out],
        scratch_shapes=[
            pltpu.VMEM(s, jnp.float32) if isinstance(s, tuple) else s for s in scratch
        ],
        cost_estimate=cost(us),
        compiler_params=pltpu.CompilerParams(vmem_limit_bytes=12 * 2**20),
    )(*args)


def split_kernel(a_ref, b_ref, out):
    rows = out.shape[1]
    for block in range(out.shape[0]):
        at = slice(rows * block, rows * (block + 1))
        out[block] = a_ref[at] + b_ref[at]


def total_kernel(parts_ref, out):
    at = 2 * lax.rem(lax.axis_index("y"), 2) + lax.axis_index("c")
    total = parts_ref[at]
    for k in range(1, 8):
        total = total + parts_ref[at + 4 * k]
    out[...] = total


def half_kernel(parts_ref, out):
    out[...] = jnp.sum(parts_ref[...], axis=0)


def gram_kernel(length_ref, a_ref, b_ref, w_ref, *refs):
    out, held = refs[-2:]
    x, y = lax.axis_index("x"), lax.axis_index("y")
    total = a_ref[...] + b_ref[...]
    slots = lax.broadcasted_iota(jnp.int32, w_ref.shape, 1)
    weights = jnp.where(slots < length_ref[y], w_ref[...], 0.0)
    inputs = (total[:, :64].T * weights).reshape(32, 2, -1)
    right, rest = two_terms(total[:, 64:])
    for odd in range(2):
        high, low = two_terms(inputs[:, odd])

        def dot(left, other):
            return jnp.dot(left, other, preferred_element_type=jnp.float32)

        held[:, 64 * odd : 64 * (odd + 1)] = dot(high, right) + (
            dot(low, right) + dot(high, rest)
        )
    for zl in range(4):
        piece = jnp.concatenate(
            [held[pl.ds(lax.rem(x + k, 4) * 8 + zl * 2, 2)] for k in (0, 3, 1, 2)], axis=0
        )
        for core in range(2):
            for y in range(4):
                out[16 * core + 4 * zl + y] = piece


def two_terms(value):
    high = value.astype(jnp.bfloat16)
    return high, (value - high.astype(jnp.float32)).astype(jnp.bfloat16)


def times(left, right):
    return lax.dot_general(
        left, right, (((1,), (1,)), ((), ())), preferred_element_type=jnp.float32
    )


def image_kernel(rows_ref, *refs):
    hess, out = refs[:4], refs[4]
    for layer in range(2):
        at = slice(16 * layer, 16 * (layer + 1))
        total = 0.0
        for k in range(4):
            rows = [rows_ref[at, 2 * k + half, :] for half in range(2)]
            high, low = two_terms(jnp.concatenate(rows, axis=1))
            right, rest = two_terms(hess[k][layer])
            both = times(jnp.concatenate([high, low], axis=0), right)
            total = total + (both[:16] + (both[16:] + times(high, rest)))
        out[at] = total


def score_kernel(*refs):
    images, queries, out = refs[:4], refs[4:8], refs[8]
    x = lax.axis_index("x")
    image = images[0][...] + images[1][...] + images[2][...] + images[3][...]
    high, low = two_terms(image)
    for k, step in enumerate((0, 3, 1, 2)):
        part = 0.0
        for layer in range(2):
            at = slice(16 * layer, 16 * (layer + 1))
            part = part + times(
                jnp.concatenate([high[at], low[at]], axis=0), queries[k][layer]
            )
        part = part[:16] + part[16:]
        for zl in range(4):
            out[4 * lax.rem(x + step, 4) + zl] = part[4 * zl : 4 * zl + 4]


def place_kernel(a_ref, b_ref, out):
    here = lax.axis_index("zl") >> 1
    out[...] = jnp.zeros_like(out)
    for block in range(4):
        for zl in range(4):
            out[16 * (block & 1) + 8 * here + 4 * (block >> 1) + zl] = a_ref[4 * block + zl] + b_ref[4 * block + zl]


def per_device(
    acts, out_grads, token_ids, lengths, token_weight, proj_in, proj_out, hess_inv, queries
):
    z, y, c = where()
    proj_in = jnp.swapaxes(proj_in, 1, 2)
    proj_out = jnp.swapaxes(proj_out, 1, 2)
    others = (1, 2, 3)

    other = project((1 - c)[None], acts, out_grads, proj_in, proj_out, 57)
    theirs = to_core(other)
    hess = [hess_inv, to_x(hess_inv, 1), to_x(hess_inv, -1)]
    query = [queries, to_x(queries, 1), to_x(queries, -1)]
    hess.append(to_x(hess_inv, 2))
    query.append(to_x(queries, 2))
    mine = project(c[None], acts, out_grads, proj_in, proj_out, 48)

    (blocks,) = call(split_kernel, [(4, 256, 128)], mine, theirs)
    blocks = lax.all_to_all(blocks, "y", 0, 0, tiled=True)

    ids = lax.dynamic_index_in_dim(token_ids, y, 0, keepdims=False)
    weights = token_weight.at[ids].get(mode="promise_in_bounds")[None]

    (half,) = call(half_kernel, [(256, 128)], blocks)
    (grams,) = call(
        gram_kernel,
        [(32, 8, 128)],
        lengths,
        half,
        to_z(half),
        weights,
        scratch=[(32, 128)],
        specs=[SMEM] + [VMEM] * 3,
    )
    grams = lax.all_to_all(grams, ("c", "zl", "y"), 0, 0, tiled=True)
    (image,) = call(image_kernel, [(32, 256)], grams, *hess)
    images = [image] + [to_zl(image, k) for k in others]
    (parts,) = call(score_kernel, [(16, 4, 256)], *images, *query)
    (parts,) = call(place_kernel, [(32, 4, 256)], parts, to_core(parts))
    parts = lax.all_to_all(parts, ("y", "z", "zl"), 0, 0, tiled=True)
    (scores,) = call(total_kernel, [(4, 256)], parts)
    return scores


def solution(mesh):
    mesh = jax.sharding.Mesh(mesh.devices.reshape(4, 4, 2, 4, 2), AXES)
    in_specs = (
        P(None, DP, MP),
        P(None, DP, MP),
        P(DP, None),
        P(DP),
        P(),
        P(None, MP, None),
        P(None, MP, None),
        P(None, MP, DP),
        P(None, DP, MP),
    )
    return jax.shard_map(
        per_device, mesh=mesh, in_specs=in_specs, out_specs=P(DP, MP), check_vma=False
    )
```
